32 devices in a mesh: blk: 16 (over z, y, core), rows: 2 (over x).
Axes of the slice: x: 2, y: 2, z: 4, core: 2. Of those that a mesh axis runs over, the one named last changes fastest.
Arguments:
- coeffs: bfloat16 [64, 12288, 384], P('blk', 'rows'), may hold values from -0.09765625 to 0.09765625
- counts: int32 [64], P('blk'), may hold values from 96 to 384, as said below
- kinetic: float32 [64], replicated, may hold values from -4 to 4
- pair_table: int32 [64, 4], P('blk'), may hold values from 0 to 63
- trial_vecs: bfloat16 [64, 384, 128], P('blk', 'rows'), may hold values from -6 to 6
- owner_map: int32 [2], replicated, may hold values from 0 to 1, each once
Outputs:
- product: bfloat16 [64, 384, 128], P('blk', 'rows')
The draws below stay inside these ranges and needn't reach their ends.
Inputs may be any that keep to these rules, and one draw needn't show every extreme that they name: `counts`: some angular point keeps all 384 eigenvectors.
All inputs are finite; a program needn't handle non-finite values.
Results may differ from the reference program's by a relative error of at most 0.012.
Values may be sent and summed in bfloat16 or wider, within the bound.
No kernel may reach another device: no remote copies, remote signals or barrier semaphores. Data moves between devices by JAX's collectives and lax.ppermute only.
A program may use at most 128 MiB of HBM per device.

```python
import jax
import jax.numpy as jnp
from jax import lax

R = 12288
KMAX = 384
V = 128
NKIN = 64
ANG_DEV = 4
NANG = 64
N_ROWS = 2


def draw_counts(key, part):
    key = jax.random.fold_in(key, 11)
    first, second = jax.random.split(key)
    values = jax.random.randint(first, (NANG,), KMAX // 4, KMAX + 1)
    where = jax.random.randint(second, (), 0, NANG)
    return values.at[where].set(KMAX).astype(jnp.int32)


def place_ends(drawn, own_key, least, top_value):
    longest = drawn.shape.index(max(drawn.shape))
    spots = []
    for shift in (0, 1):
        where = [jax.random.randint(jax.random.fold_in(own_key, axis), (), 0, length) for axis, length in enumerate(drawn.shape)]
        where[longest] = (where[longest] + shift) % drawn.shape[longest]
        spots.append(tuple(where))
    return drawn.at[spots[0]].set(least).at[spots[1]].set(top_value)


def block_scale(key, extent, cuts, low, largest):
    def one(dim, shards_of):
        draws = jax.random.uniform(jax.random.fold_in(jax.random.fold_in(key, 6), dim), (shards_of,), jnp.float32, low / len(cuts), largest / len(cuts))
        return jnp.repeat(jnp.exp(draws), extent[dim] // shards_of).reshape((-1,) + (1,) * (len(extent) - dim - 1))

    factor_of = one(*cuts[0])
    for cut in cuts[1:]:
        factor_of = factor_of * one(*cut)
    return factor_of


def gaussian(stream_key, dims, deviation, reach, pieces=(), held_as=jnp.bfloat16):
    values = jax.random.normal(stream_key, dims, jnp.float32) * deviation
    if len(pieces) > 0:
        values = block_scale(stream_key, dims, pieces, -0.22, 0.18) * values
    return jnp.clip(values, min=-reach, max=reach).astype(held_as)


def setup_inputs(seed: int = 0) -> dict:
    seeds = jax.random.split(jax.random.key(seed), 7)
    return {
        "coeffs": gaussian(seeds[0], (NANG, R, KMAX), ((3 * R * KMAX) ** -0.25), 0.09765625, ((0, 16), (1, 2))),
        "counts": draw_counts(jax.random.fold_in(seeds[6], 71), 0),
        "kinetic": gaussian(seeds[2], (NKIN,), 1.0, 4.0, (), jnp.float32),
        "pair_table": place_ends(jax.random.randint(seeds[3], (NANG, ANG_DEV), 0, NKIN), jax.random.fold_in(seeds[3], 1), 0, NKIN - 1).astype(jnp.int32),
        "trial_vecs": gaussian(seeds[4], (NANG, KMAX, V), 1.0, 6.0, ((0, 16), (1, 2))),
        "owner_map": jax.random.permutation(seeds[5], N_ROWS).astype(jnp.int32),
    }


def reference(coeffs, counts, kinetic, pair_table, trial_vecs, owner_map):
    column = jnp.arange(KMAX, dtype=jnp.int32)
    keep_mask = (column[None, :] < counts[:, None]).astype(jnp.bfloat16)
    masked = coeffs * keep_mask[:, None, :]
    previous = jnp.roll(masked, ANG_DEV, axis=0)
    prev_trial = jnp.roll(trial_vecs, ANG_DEV, axis=0)
    kin_scale = kinetic[pair_table]
    slab = R // N_ROWS
    groups = NANG // ANG_DEV

    def one_group(index):
        start = (index * ANG_DEV).astype(jnp.int32)
        left = lax.dynamic_slice_in_dim(masked, start, ANG_DEV, 0).reshape(ANG_DEV, N_ROWS, slab, KMAX)
        right = lax.dynamic_slice_in_dim(previous, start, ANG_DEV, 0).reshape(ANG_DEV, N_ROWS, slab, KMAX)
        scales = lax.dynamic_slice_in_dim(kin_scale, start, ANG_DEV, 0)
        vectors = lax.dynamic_slice_in_dim(prev_trial, start, ANG_DEV, 0).astype(jnp.float32)
        partial_value = jnp.einsum("iprk,jprl->pijkl", left.astype(jnp.float32), right.astype(jnp.float32), precision=lax.Precision.HIGHEST)
        tile = jnp.sum(partial_value.astype(jnp.bfloat16).astype(jnp.float32), axis=0)
        scaled = tile * scales[:, :, None, None]
        return jnp.einsum("ijkl,jlv->ikv", scaled, vectors, precision=lax.Precision.HIGHEST)

    result = lax.map(one_group, jnp.arange(groups, dtype=jnp.int32))
    result = result.reshape(NANG, N_ROWS, KMAX // N_ROWS, V)
    result = jnp.take(result, owner_map, axis=1)
    return result.reshape(NANG, KMAX, V).astype(jnp.bfloat16)
```

```python
import functools

import jax
import jax.numpy as jnp
from jax import lax
from jax.experimental import pallas as pl
from jax.experimental.pallas import tpu as pltpu
from jax.sharding import PartitionSpec as P

VMEM_LIMIT = 48 * 1024 * 1024


def shifted(block, axis, distance):
    devices = range(lax.axis_size(axis))
    route = [(i, (i + distance) % len(devices)) for i in devices]
    return lax.ppermute(block, axis, route)


def block_rows(length):
    for rows in (768, 512, 384, 256, 192, 128, 96, 64, 48, 32, 16):
        if length % rows == 0:
            return rows
    return length


def produce_kernel(kin_ref, sets_ref, vectors_ref, out_ref):
    points = sets_ref.shape[0]
    products = [
        jnp.dot(sets_ref[j], vectors_ref[j], preferred_element_type=jnp.float32)
        for j in range(points)
    ]
    for a in range(out_ref.shape[0]):
        total = kin_ref[a, 0] * products[0]
        for j in range(1, points):
            total += kin_ref[a, j] * products[j]
        out_ref[a] = total.astype(out_ref.dtype)


def produce(sets, vectors, kin, start, length):
    points, _, kept = sets.shape
    width = vectors.shape[2]
    rows = block_rows(length)
    first = start // rows
    return pl.pallas_call(
        produce_kernel,
        grid=(length // rows,),
        in_specs=[
            pl.BlockSpec(memory_space=pltpu.SMEM),
            pl.BlockSpec((points, rows, kept), lambda i: (0, first + i, 0)),
            pl.BlockSpec((points, kept, width), lambda i: (0, 0, 0)),
        ],
        out_specs=pl.BlockSpec((points, rows, width), lambda i: (0, i, 0)),
        out_shape=jax.ShapeDtypeStruct((points, length, width), jnp.bfloat16),
        compiler_params=pltpu.CompilerParams(vmem_limit_bytes=VMEM_LIMIT),
        cost_estimate=pl.CostEstimate(
            flops=2 * points * length * kept * width,
            bytes_accessed=2 * points * length * (kept + width),
            transcendentals=0,
        ),
    )(kin, sets, vectors)


def consume_kernel(sets_ref, arrived_ref, before_ref, out_ref):
    @pl.when(pl.program_id(0) == 0)
    def _():
        out_ref[...] = before_ref[...]

    for a in range(out_ref.shape[0]):
        out_ref[a] += lax.dot_general(
            arrived_ref[a],
            sets_ref[a],
            (((0,), (0,)), ((), ())),
            preferred_element_type=jnp.float32,
        )


def consume(sets, arrived, before, start):
    points, _, kept = sets.shape
    _, length, width = arrived.shape
    rows = block_rows(length)
    first = start // rows
    return pl.pallas_call(
        consume_kernel,
        grid=(length // rows,),
        in_specs=[
            pl.BlockSpec((points, rows, kept), lambda i: (0, first + i, 0)),
            pl.BlockSpec((points, rows, width), lambda i: (0, i, 0)),
            pl.BlockSpec((points, width, kept), lambda i: (0, 0, 0)),
        ],
        out_specs=pl.BlockSpec((points, width, kept), lambda i: (0, 0, 0)),
        out_shape=jax.ShapeDtypeStruct((points, width, kept), jnp.float32),
        compiler_params=pltpu.CompilerParams(vmem_limit_bytes=VMEM_LIMIT),
        cost_estimate=pl.CostEstimate(
            flops=2 * points * length * kept * width,
            bytes_accessed=2 * points * length * (kept + width),
            transcendentals=0,
        ),
    )(sets, arrived, before)


def per_device(coeffs, counts, kinetic, pair_table, trial_vecs, owner_map):
    points, radial, kept = coeffs.shape
    share, width = trial_vecs.shape[1:]
    blocks = lax.axis_size("rows")
    me = lax.axis_index("rows")

    table_index = jnp.arange(kinetic.shape[0], dtype=jnp.int32)
    one_hot = pair_table[:, :, None] == table_index[None, None, :]
    kin_own = jnp.sum(jnp.where(one_hot, kinetic[None, None, :], 0.0), axis=2)
    kin_next = shifted(kin_own, "blk", -1)

    pieces = [trial_vecs] + [shifted(trial_vecs, "rows", d) for d in range(1, blocks)]
    if blocks == 2:
        low = jnp.where(me == 0, pieces[0], pieces[1])
        high = jnp.where(me == 0, pieces[1], pieces[0])
        vectors = jnp.concatenate([low, high], axis=1)
    else:
        stacked = jnp.stack(pieces, axis=1)
        order = (me - jnp.arange(blocks)) % blocks
        vectors = jnp.take(stacked, order, axis=1).reshape(points, kept, width)
    column = jnp.arange(kept, dtype=jnp.int32)
    keep = column[None, :] < counts[:, None]
    vectors = jnp.where(keep[:, :, None], vectors, jnp.zeros((), vectors.dtype))

    step = radial // 8
    bounds = [(0, step), (step, step), (2 * step, 2 * step), (4 * step, 2 * step), (6 * step, step), (7 * step, step)]
    sent = [shifted(produce(coeffs, vectors, kin_next, s, n), "blk", 1) for s, n in bounds]
    total = jnp.zeros((points, width, kept), jnp.float32)
    for (s, n), z in zip(bounds, sent):
        total = consume(coeffs, z, total, s)

    result = jnp.where(keep[:, :, None], total.transpose(0, 2, 1), 0.0)

    def block_of(index):
        return lax.dynamic_slice_in_dim(result, owner_map[index] * share, share, 1)

    final = block_of(me)
    for d in range(1, blocks):
        out = block_of((me + d) % blocks).astype(jnp.bfloat16)
        final += shifted(out, "rows", d).astype(jnp.float32)
    return final.astype(jnp.bfloat16)


def solution(mesh):
    in_specs = (P("blk", "rows", None), P("blk"), P(), P("blk", None), P("blk", "rows", None), P())
    out_specs = P("blk", "rows", None)
    return jax.shard_map(
        per_device, mesh=mesh, in_specs=in_specs, out_specs=out_specs, check_vma=False
    )
```

```python
import functools

import jax
import jax.numpy as jnp
from jax import lax
from jax.experimental import pallas as pl
from jax.experimental.pallas import tpu as pltpu
from jax.sharding import PartitionSpec as P

VMEM_LIMIT = 50 * 1024 * 1024
SMEM = pl.BlockSpec(memory_space=pltpu.SMEM)
VMEM = pl.BlockSpec(memory_space=pltpu.VMEM)
ORDER = pl.BlockSpec(memory_space=pl.ANY)
CHEAP = pl.CostEstimate(flops=1, bytes_accessed=1, transcendentals=0)


def shifted(block, axis, distance):
    devices = range(lax.axis_size(axis))
    route = [(i, (i + distance) % len(devices)) for i in devices]
    return lax.ppermute(block, axis, route)


def after(value, *others):
    return lax.optimization_barrier((value, *others))[0]


def params():
    return pltpu.CompilerParams(vmem_limit_bytes=VMEM_LIMIT)


def contract_rows(left, right):
    return lax.dot_general(
        left, right, (((0,), (0,)), ((), ())), preferred_element_type=jnp.float32
    )


def fill(vectors, pieces, count, me):
    share = pieces[0].shape[0]
    blocks = len(pieces)
    for d, piece in enumerate(pieces):
        start = pl.multiple_of(lax.rem(me + (blocks - d), blocks) * share, 16)
        row = start + lax.broadcasted_iota(jnp.int32, piece.shape, 0)
        kept = jnp.where(row < count, piece.astype(jnp.float32), 0.0)
        vectors[pl.ds(start, share), :] = kept.astype(vectors.dtype)


def apply_kernel(first, _, counts_ref, me_ref, sets_ref, own_ref, *rest):
    *others, out_ref, vectors = rest
    i = pl.program_id(0)
    fill(vectors, [r[0] for r in (own_ref, *others)], counts_ref[first + i], me_ref[0])
    out_ref[0] = jnp.dot(
        sets_ref[0], vectors[...], preferred_element_type=jnp.float32
    ).astype(out_ref.dtype)


def apply_first(sets, own, others, counts, me, start, rows):
    kept = sets.shape[2]
    share, width = own.shape[1:]
    block = rows // 2
    skip = start // block

    def kernel(counts_ref, me_ref, sets_ref, own_ref, *rest):
        *pieces, out_ref, vectors = rest

        @pl.when(pl.program_id(0) == 0)
        def _():
            fill(vectors, [r[0] for r in (own_ref, *pieces)], counts_ref[0], me_ref[0])

        out_ref[0] = jnp.dot(
            sets_ref[0], vectors[...], preferred_element_type=jnp.float32
        ).astype(out_ref.dtype)

    return pl.pallas_call(
        kernel,
        grid=(2,),
        in_specs=[SMEM, SMEM, pl.BlockSpec((1, block, kept), lambda i: (0, skip + i, 0))]
        + [pl.BlockSpec((1, share, width), lambda i: (0, 0, 0))] * (1 + len(others)),
        out_specs=pl.BlockSpec((1, block, width), lambda i: (0, i, 0)),
        out_shape=jax.ShapeDtypeStruct((1, rows, width), jnp.bfloat16),
        scratch_shapes=[pltpu.VMEM((kept, width), jnp.bfloat16)],
        compiler_params=params(),
        cost_estimate=CHEAP,
        name="apply_first",
    )(counts, me, sets, own, *others)


def apply_rest(sets, own, others, earlier, counts, me, start, rows):
    points, _, kept = sets.shape
    share, width = own.shape[1:]
    own_spec = pl.BlockSpec((1, share, width), lambda i: (i + 1, 0, 0))
    skip = start // rows
    return pl.pallas_call(
        functools.partial(apply_kernel, 1),
        grid=(points - 1,),
        in_specs=[ORDER, SMEM, SMEM, pl.BlockSpec((1, rows, kept), lambda i: (i + 1, skip, 0))]
        + [own_spec] * (1 + len(others)),
        out_specs=pl.BlockSpec((1, rows, width), lambda i: (i, 0, 0)),
        out_shape=jax.ShapeDtypeStruct((points - 1, rows, width), jnp.bfloat16),
        scratch_shapes=[pltpu.VMEM((kept, width), jnp.bfloat16)],
        compiler_params=params(),
        cost_estimate=CHEAP,
        name="apply_rest",
    )(earlier, counts, me, sets, own, *others)


def combine(sets, own, others, counts, me, kin, length, block, tail):
    points, _, kept = sets.shape
    share, width = own.shape[1:]
    steps = length // block
    body = steps - tail // block
    peers = len(others)

    def kernel(counts_ref, me_ref, kin_ref, sets_ref, own_ref, *refs):
        other_refs, outs, vectors = refs[:peers], refs[peers:-1], refs[-1]
        i = pl.program_id(0)

        @pl.when(i == 0)
        def _():
            for j in range(points):
                pieces = [r[j] for r in (own_ref, *other_refs)]
                fill(vectors.at[j], pieces, counts_ref[j], me_ref[0])

        products = [
            jnp.dot(sets_ref[j], vectors[j], preferred_element_type=jnp.float32)
            for j in range(points)
        ]

        def mixed(a):
            total = kin_ref[a, 0] * products[0]
            for j in range(1, points):
                total += kin_ref[a, j] * products[j]
            return total.astype(jnp.bfloat16)

        for a in range(points - 1):
            outs[a][...] = mixed(a)
        last = mixed(points - 1)

        @pl.when(i < body)
        def _():
            outs[points - 1][...] = last

        @pl.when(i >= body)
        def _():
            outs[points][...] = last

    whole = pl.BlockSpec((block, width), lambda i: (i, 0))
    return pl.pallas_call(
        kernel,
        grid=(steps,),
        in_specs=[SMEM, SMEM, SMEM, pl.BlockSpec((points, block, kept), lambda i: (0, i, 0))]
        + [VMEM] * (1 + peers),
        out_specs=[whole] * (points - 1)
        + [
            pl.BlockSpec((block, width), lambda i: (jnp.minimum(i, body - 1), 0)),
            pl.BlockSpec((block, width), lambda i: (jnp.maximum(i - body, 0), 0)),
        ],
        out_shape=[jax.ShapeDtypeStruct((length, width), jnp.bfloat16)] * (points - 1)
        + [
            jax.ShapeDtypeStruct((length - tail, width), jnp.bfloat16),
            jax.ShapeDtypeStruct((tail, width), jnp.bfloat16),
        ],
        scratch_shapes=[pltpu.VMEM((points, kept, width), jnp.bfloat16)],
        compiler_params=params(),
        cost_estimate=CHEAP,
        name="combine",
    )(counts, me, kin, sets, own, *others)


def collect(sets, first, rest, kin, start, rows):
    points, _, kept = sets.shape
    width = first.shape[2]
    skip = start // rows

    def kernel(kin_ref, sets_ref, first_ref, rest_ref, out_ref):
        a = pl.program_id(0)
        arrived = [first_ref[0]] + [rest_ref[j] for j in range(points - 1)]
        products = contract_rows(sets_ref[0], jnp.concatenate(arrived, axis=1))
        total = kin_ref[a, 0] * products[:, :width]
        for j in range(1, points):
            total += kin_ref[a, j] * products[:, j * width : (j + 1) * width]
        out_ref[0] = total

    return pl.pallas_call(
        kernel,
        grid=(points,),
        in_specs=[SMEM, pl.BlockSpec((1, rows, kept), lambda a: (a, skip, 0)), VMEM, VMEM],
        out_specs=pl.BlockSpec((1, kept, width), lambda a: (a, 0, 0)),
        out_shape=jax.ShapeDtypeStruct((points, kept, width), jnp.float32),
        compiler_params=params(),
        cost_estimate=CHEAP,
        name="collect",
    )(kin, sets, first, rest)


def split_blocks(total, point, counts_ref, owner_ref, me, held, own_ref, send_ref):
    blocks = owner_ref.shape[0]
    share = own_ref.shape[0]
    row = lax.broadcasted_iota(jnp.int32, total.shape, 0)
    held[...] = jnp.where(row < counts_ref[point], total, 0.0)
    for d in range(blocks):
        start = pl.multiple_of(owner_ref[lax.rem(me + d, blocks)] * share, 16)
        part = held[pl.ds(start, share), :]
        if d == 0:
            own_ref[...] = part
        else:
            send_ref[d - 1] = part.astype(send_ref.dtype)


def gather_rows(sets, arrived, before, earlier, point, block):
    kept = sets.shape[2]
    length, width = arrived.shape

    def kernel(_, sets_ref, arrived_ref, before_ref, out_ref):
        @pl.when(pl.program_id(0) == 0)
        def _():
            out_ref[...] = before_ref[0]

        out_ref[...] += contract_rows(sets_ref[0], arrived_ref[...])

    return pl.pallas_call(
        kernel,
        grid=(length // block,),
        in_specs=[
            ORDER,
            pl.BlockSpec((1, block, kept), lambda i: (point, i, 0)),
            pl.BlockSpec((block, width), lambda i: (i, 0)),
            pl.BlockSpec((1, kept, width), lambda i: (point, 0, 0)),
        ],
        out_specs=pl.BlockSpec((kept, width), lambda i: (0, 0)),
        out_shape=jax.ShapeDtypeStruct((kept, width), jnp.float32),
        compiler_params=params(),
        cost_estimate=CHEAP,
        name="gather_rows",
    )(earlier, sets, arrived, before)


def finish_rows(sets, arrived, before, earlier, counts, me, owner_map, point, block, share):
    kept = sets.shape[2]
    length, width = arrived.shape
    steps = length // block
    blocks = owner_map.shape[0]

    def kernel(_, counts_ref, me_ref, owner_ref, sets_ref, arrived_ref, before_ref, own_ref, send_ref, total, held):
        i = pl.program_id(0)

        @pl.when(i == 0)
        def _():
            total[...] = before_ref[0]

        total[...] += contract_rows(sets_ref[0], arrived_ref[...])

        @pl.when(i == steps - 1)
        def _():
            split_blocks(total[...], point, counts_ref, owner_ref, me_ref[0], held, own_ref, send_ref)

    return pl.pallas_call(
        kernel,
        grid=(steps,),
        in_specs=[
            ORDER,
            SMEM,
            SMEM,
            SMEM,
            pl.BlockSpec((1, block, kept), lambda i: (point, i, 0)),
            pl.BlockSpec((block, width), lambda i: (i, 0)),
            pl.BlockSpec((1, kept, width), lambda i: (point, 0, 0)),
        ],
        out_specs=[
            pl.BlockSpec((share, width), lambda i: (0, 0)),
            pl.BlockSpec((blocks - 1, share, width), lambda i: (0, 0, 0)),
        ],
        out_shape=[
            jax.ShapeDtypeStruct((share, width), jnp.float32),
            jax.ShapeDtypeStruct((blocks - 1, share, width), jnp.bfloat16),
        ],
        scratch_shapes=[pltpu.VMEM((kept, width), jnp.float32)] * 2,
        compiler_params=params(),
        cost_estimate=CHEAP,
        name="finish_rows",
    )(earlier, counts, me, owner_map, sets, arrived, before)


def finish_last(sets, arrived, before, earlier, counts, me, owner_map, point, share):
    kept = sets.shape[1]
    width = arrived.shape[1]
    blocks = owner_map.shape[0]

    def kernel(_, counts_ref, me_ref, owner_ref, sets_ref, arrived_ref, before_ref, own_ref, send_ref, held):
        total = before_ref[...] + contract_rows(sets_ref[...], arrived_ref[...])
        split_blocks(total, point, counts_ref, owner_ref, me_ref[0], held, own_ref, send_ref)

    return pl.pallas_call(
        kernel,
        in_specs=[ORDER] + [SMEM] * 3 + [VMEM] * 3,
        out_specs=[VMEM, VMEM],
        out_shape=[
            jax.ShapeDtypeStruct((share, width), jnp.float32),
            jax.ShapeDtypeStruct((blocks - 1, share, width), jnp.bfloat16),
        ],
        scratch_shapes=[pltpu.VMEM((kept, width), jnp.float32)],
        compiler_params=params(),
        cost_estimate=CHEAP,
        name="finish_last",
    )(earlier, counts, me, owner_map, sets, arrived, before)


def place_last(ready, own, others):
    points, share, width = ready.shape

    def kernel(_, own_ref, *rest):
        *other_refs, out_ref = rest
        total = own_ref[...]
        for r in other_refs:
            total += r[...].astype(jnp.float32)
        out_ref[0] = total.astype(out_ref.dtype)

    return pl.pallas_call(
        kernel,
        grid=(1,),
        in_specs=[ORDER] + [VMEM] * (1 + len(others)),
        out_specs=pl.BlockSpec((1, share, width), lambda i: (points - 1, 0, 0)),
        out_shape=jax.ShapeDtypeStruct(ready.shape, ready.dtype),
        input_output_aliases={0: 0},
        compiler_params=params(),
        cost_estimate=CHEAP,
        name="place_last",
    )(ready, own, *others)


def exchange(own, send):
    for d in range(1, send.shape[0] + 1):
        own += shifted(send[d - 1], "rows", d).astype(jnp.float32)
    return own


def per_device(coeffs, counts, kinetic, pair_table, trial_vecs, owner_map):
    points, radial, kept = coeffs.shape
    share, width = trial_vecs.shape[1:]
    blocks = owner_map.shape[0]
    me = lax.axis_index("rows").astype(jnp.int32).reshape(1)
    unit = radial // 12
    plain, tail = 4 * unit, unit
    mixed_rows = radial - plain
    peers = range(1, blocks)

    first_own = trial_vecs[:1]
    first_vectors = [shifted(first_own, "rows", d) for d in peers]
    vectors = [shifted(trial_vecs, "rows", d) for d in peers]

    first = apply_first(coeffs, first_own, first_vectors, counts, me, mixed_rows, plain)
    first_sent = shifted(first, "blk", 1)

    table_index = jnp.arange(kinetic.shape[0], dtype=jnp.int32)
    one_hot = pair_table[:, :, None] == table_index[None, None, :]
    kin_own = jnp.sum(jnp.where(one_hot, kinetic[None, None, :], 0.0), axis=2)
    rest = apply_rest(coeffs, trial_vecs, vectors, first, counts, me, mixed_rows, plain)
    rest_sent = shifted(rest, "blk", 1)
    kin_next = shifted(after(kin_own, rest, first_sent), "blk", -1)
    mixed = combine(
        coeffs, trial_vecs, vectors, counts, me, kin_next, mixed_rows, unit, tail
    )
    mixed_sent = []
    previous = rest
    for z in mixed:
        z = after(z, previous)
        previous = z
        mixed_sent.append(shifted(z, "blk", 1))

    base = collect(coeffs, first_sent, rest_sent, kin_own, mixed_rows, plain)
    done = []
    earlier = first_sent
    for a in range(points - 1):
        own, send = finish_rows(
            coeffs, mixed_sent[a], base, earlier, counts, me, owner_map, a, mixed_rows // 2, share
        )
        earlier = own
        done.append(exchange(own, send))
    last = points - 1
    total = gather_rows(coeffs, mixed_sent[last], base, earlier, last, mixed_rows - tail)
    ready = jnp.stack(done + done[:1]).astype(jnp.bfloat16)
    own, send = finish_last(
        coeffs[last, mixed_rows - tail : mixed_rows], mixed_sent[points], total, ready, counts, me, owner_map, last, share
    )
    return place_last(ready, own, [shifted(send[d - 1], "rows", d) for d in peers])


def solution(mesh):
    in_specs = (P("blk", "rows", None), P("blk"), P(), P("blk", None), P("blk", "rows", None), P())
    out_specs = P("blk", "rows", None)
    return jax.shard_map(
        per_device, mesh=mesh, in_specs=in_specs, out_specs=out_specs, check_vma=False
    )
```

```python
import functools

import jax
import jax.numpy as jnp
from jax import lax
from jax.experimental import pallas as pl
from jax.experimental.pallas import tpu as pltpu
from jax.sharding import PartitionSpec as P

VMEM_LIMIT = 50 * 1024 * 1024
SMEM = pl.BlockSpec(memory_space=pltpu.SMEM)
VMEM = pl.BlockSpec(memory_space=pltpu.VMEM)
ORDER = pl.BlockSpec(memory_space=pl.ANY)
CHEAP = pl.CostEstimate(flops=1, bytes_accessed=1, transcendentals=0)


def shifted(block, axis, distance):
    devices = range(lax.axis_size(axis))
    route = [(i, (i + distance) % len(devices)) for i in devices]
    return lax.ppermute(block, axis, route)


def after(value, *others):
    return lax.optimization_barrier((value, *others))[0]


def params():
    return pltpu.CompilerParams(vmem_limit_bytes=VMEM_LIMIT)


def contract_rows(left, right):
    return lax.dot_general(
        left, right, (((0,), (0,)), ((), ())), preferred_element_type=jnp.float32
    )


def fill(vectors, pieces, count, me):
    share = pieces[0].shape[0]
    blocks = len(pieces)
    for d, piece in enumerate(pieces):
        start = pl.multiple_of(lax.rem(me + (blocks - d), blocks) * share, 16)
        row = start + lax.broadcasted_iota(jnp.int32, piece.shape, 0)
        kept = jnp.where(row < count, piece.astype(jnp.float32), 0.0)
        vectors[pl.ds(start, share), :] = kept.astype(vectors.dtype)


def parcels(points):
    return 1, points - 1


def place(point, sizes):
    for index, size in enumerate(sizes):
        if point < size:
            return index, point
        point -= size
    raise ValueError(point)


def parted(vectors):
    points, share, width = vectors.shape
    sizes = parcels(points)

    def kernel(vectors_ref, *outs):
        start = 0
        for out, size in zip(outs, sizes):
            out[...] = vectors_ref[start : start + size]
            start += size

    return pl.pallas_call(
        kernel,
        in_specs=[VMEM],
        out_specs=[VMEM] * len(sizes),
        out_shape=[jax.ShapeDtypeStruct((size, share, width), vectors.dtype) for size in sizes],
        compiler_params=params(),
        cost_estimate=CHEAP,
        name="parted",
    )(vectors)


def apply_first(sets, pieces, facts, start, rows):
    kept = sets.shape[2]
    width = pieces[0].shape[2]
    block = rows // 2
    skip = start // block

    def kernel(facts_ref, sets_ref, *rest):
        *piece_refs, out_ref, vectors = rest

        @pl.when(pl.program_id(0) == 0)
        def _():
            fill(vectors, [r[0] for r in piece_refs], facts_ref[1], facts_ref[0])

        out_ref[0] = jnp.dot(
            sets_ref[0], vectors[...], preferred_element_type=jnp.float32
        ).astype(out_ref.dtype)

    return pl.pallas_call(
        kernel,
        grid=(2,),
        in_specs=[SMEM, pl.BlockSpec((1, block, kept), lambda i: (0, skip + i, 0))]
        + [VMEM] * len(pieces),
        out_specs=pl.BlockSpec((1, block, width), lambda i: (0, i, 0)),
        out_shape=jax.ShapeDtypeStruct((1, rows, width), jnp.bfloat16),
        scratch_shapes=[pltpu.VMEM((kept, width), jnp.bfloat16)],
        compiler_params=params(),
        cost_estimate=pl.CostEstimate(flops=10**9, bytes_accessed=10**6, transcendentals=0),
        name="apply_first",
    )(facts, sets, *pieces)


def apply_rest(sets, pieces, earlier, facts, start, rows):
    points, _, kept = sets.shape
    width = pieces[0][0].shape[2]
    blocks = len(pieces[0])
    skip = start // rows
    sizes = parcels(points)

    def kernel(_, facts_ref, sets_ref, *rest):
        *piece_refs, out_ref, vectors = rest
        for j in range(1, points):

            @pl.when(pl.program_id(0) == j - 1)
            def _():
                index, row = place(j, sizes)
                mine = piece_refs[index * blocks :][:blocks]
                fill(vectors, [r[row] for r in mine], facts_ref[1 + j], facts_ref[0])

        out_ref[0] = jnp.dot(
            sets_ref[0], vectors[...], preferred_element_type=jnp.float32
        ).astype(out_ref.dtype)

    return pl.pallas_call(
        kernel,
        grid=(points - 1,),
        in_specs=[ORDER, SMEM, pl.BlockSpec((1, rows, kept), lambda i: (i + 1, skip, 0))]
        + [VMEM] * (len(sizes) * blocks),
        out_specs=pl.BlockSpec((1, rows, width), lambda i: (i, 0, 0)),
        out_shape=jax.ShapeDtypeStruct((points - 1, rows, width), jnp.bfloat16),
        scratch_shapes=[pltpu.VMEM((kept, width), jnp.bfloat16)],
        compiler_params=params(),
        cost_estimate=CHEAP,
        name="apply_rest",
    )(earlier, facts, sets, *sum(pieces, []))


def combine(sets, pieces, facts, kin, length, block, tail):
    points, _, kept = sets.shape
    width = pieces[0][0].shape[2]
    sizes = parcels(points)
    steps = length // block
    body = steps - tail // block
    blocks = len(pieces[0])

    def kernel(facts_ref, kin_ref, sets_ref, *refs):
        used = len(sizes) * blocks
        piece_refs = refs[:used]
        outs, vectors = refs[used:-1], refs[-1]
        i = pl.program_id(0)

        @pl.when(i == 0)
        def _():
            for j in range(points):
                index, row = place(j, sizes)
                mine = piece_refs[index * blocks :][:blocks]
                fill(vectors.at[j], [r[row] for r in mine], facts_ref[1 + j], facts_ref[0])

        products = [
            jnp.dot(sets_ref[j], vectors[j], preferred_element_type=jnp.float32)
            for j in range(points)
        ]

        def mixed(a):
            total = kin_ref[a, 0] * products[0]
            for j in range(1, points):
                total += kin_ref[a, j] * products[j]
            return total.astype(jnp.bfloat16)

        for a in range(points - 1):
            outs[a][...] = mixed(a)
        last = mixed(points - 1)

        @pl.when(i < body)
        def _():
            outs[points - 1][...] = last

        @pl.when(i >= body)
        def _():
            outs[points][...] = last

    whole = pl.BlockSpec((block, width), lambda i: (i, 0))
    return pl.pallas_call(
        kernel,
        grid=(steps,),
        in_specs=[SMEM, SMEM, pl.BlockSpec((points, block, kept), lambda i: (0, i, 0))]
        + [VMEM] * (len(sizes) * blocks),
        out_specs=[whole] * (points - 1)
        + [
            pl.BlockSpec((block, width), lambda i: (jnp.minimum(i, body - 1), 0)),
            pl.BlockSpec((block, width), lambda i: (jnp.maximum(i - body, 0), 0)),
        ],
        out_shape=[jax.ShapeDtypeStruct((length, width), jnp.bfloat16)] * (points - 1)
        + [
            jax.ShapeDtypeStruct((length - tail, width), jnp.bfloat16),
            jax.ShapeDtypeStruct((tail, width), jnp.bfloat16),
        ],
        scratch_shapes=[pltpu.VMEM((points, kept, width), jnp.bfloat16)],
        compiler_params=params(),
        cost_estimate=CHEAP,
        name="combine",
    )(facts, kin, sets, *sum(pieces, []))


def collect(sets, first, rest, kin, start, rows):
    points, _, kept = sets.shape
    width = first.shape[2]
    skip = start // rows

    def kernel(kin_ref, sets_ref, first_ref, rest_ref, out_ref):
        a = pl.program_id(0)
        arrived = [first_ref[0]] + [rest_ref[j] for j in range(points - 1)]
        products = contract_rows(sets_ref[0], jnp.concatenate(arrived, axis=1))
        total = kin_ref[a, 0] * products[:, :width]
        for j in range(1, points):
            total += kin_ref[a, j] * products[:, j * width : (j + 1) * width]
        out_ref[0] = total

    return pl.pallas_call(
        kernel,
        grid=(points,),
        in_specs=[SMEM, pl.BlockSpec((1, rows, kept), lambda a: (a, skip, 0)), VMEM, VMEM],
        out_specs=pl.BlockSpec((1, kept, width), lambda a: (a, 0, 0)),
        out_shape=jax.ShapeDtypeStruct((points, kept, width), jnp.float32),
        compiler_params=params(),
        cost_estimate=CHEAP,
        name="collect",
    )(kin, sets, first, rest)


def split_blocks(total, point, points, facts_ref, held, own_ref, send_ref):
    blocks = facts_ref.shape[0] - 1 - points
    share = own_ref.shape[0]
    row = lax.broadcasted_iota(jnp.int32, total.shape, 0)
    held[...] = jnp.where(row < facts_ref[1 + point], total, 0.0)
    for d in range(blocks):
        start = pl.multiple_of(facts_ref[1 + points + lax.rem(facts_ref[0] + d, blocks)] * share, 16)
        part = held[pl.ds(start, share), :]
        if d == 0:
            own_ref[...] = part
        else:
            send_ref[d - 1] = part.astype(send_ref.dtype)


def gather_rows(sets, arrived, before, earlier, point, block):
    kept = sets.shape[2]
    length, width = arrived.shape

    def kernel(_, sets_ref, arrived_ref, before_ref, out_ref):
        @pl.when(pl.program_id(0) == 0)
        def _():
            out_ref[...] = before_ref[0]

        out_ref[...] += contract_rows(sets_ref[0], arrived_ref[...])

    return pl.pallas_call(
        kernel,
        grid=(length // block,),
        in_specs=[
            ORDER,
            pl.BlockSpec((1, block, kept), lambda i: (point, i, 0)),
            pl.BlockSpec((block, width), lambda i: (i, 0)),
            pl.BlockSpec((1, kept, width), lambda i: (point, 0, 0)),
        ],
        out_specs=pl.BlockSpec((kept, width), lambda i: (0, 0)),
        out_shape=jax.ShapeDtypeStruct((kept, width), jnp.float32),
        compiler_params=params(),
        cost_estimate=CHEAP,
        name="gather_rows",
    )(earlier, sets, arrived, before)


def finish_rows(sets, arrived, before, earlier, facts, point, block, share):
    points, _, kept = sets.shape
    length, width = arrived.shape
    steps = length // block
    blocks = facts.shape[0] - 1 - points

    def kernel(_, facts_ref, sets_ref, arrived_ref, before_ref, own_ref, send_ref, total, held):
        i = pl.program_id(0)

        @pl.when(i == 0)
        def _():
            total[...] = before_ref[0]

        total[...] += contract_rows(sets_ref[0], arrived_ref[...])

        @pl.when(i == steps - 1)
        def _():
            split_blocks(total[...], point, points, facts_ref, held, own_ref, send_ref)

    return pl.pallas_call(
        kernel,
        grid=(steps,),
        in_specs=[
            ORDER,
            SMEM,
            pl.BlockSpec((1, block, kept), lambda i: (point, i, 0)),
            pl.BlockSpec((block, width), lambda i: (i, 0)),
            pl.BlockSpec((1, kept, width), lambda i: (point, 0, 0)),
        ],
        out_specs=[
            pl.BlockSpec((share, width), lambda i: (0, 0)),
            pl.BlockSpec((blocks - 1, share, width), lambda i: (0, 0, 0)),
        ],
        out_shape=[
            jax.ShapeDtypeStruct((share, width), jnp.float32),
            jax.ShapeDtypeStruct((blocks - 1, share, width), jnp.bfloat16),
        ],
        scratch_shapes=[pltpu.VMEM((kept, width), jnp.float32)] * 2,
        compiler_params=params(),
        cost_estimate=CHEAP,
        name="finish_rows",
    )(earlier, facts, sets, arrived, before)


def finish_last(sets, arrived, before, earlier, facts, point, points, share):
    kept = sets.shape[1]
    width = arrived.shape[1]
    blocks = facts.shape[0] - 1 - points

    def kernel(_, facts_ref, sets_ref, arrived_ref, before_ref, own_ref, send_ref, held):
        total = before_ref[...] + contract_rows(sets_ref[...], arrived_ref[...])
        split_blocks(total, point, points, facts_ref, held, own_ref, send_ref)

    return pl.pallas_call(
        kernel,
        in_specs=[ORDER, SMEM] + [VMEM] * 3,
        out_specs=[VMEM, VMEM],
        out_shape=[
            jax.ShapeDtypeStruct((share, width), jnp.float32),
            jax.ShapeDtypeStruct((blocks - 1, share, width), jnp.bfloat16),
        ],
        scratch_shapes=[pltpu.VMEM((kept, width), jnp.float32)],
        compiler_params=params(),
        cost_estimate=CHEAP,
        name="finish_last",
    )(earlier, facts, sets, arrived, before)


def place_last(ready, own, others):
    points, share, width = ready.shape

    def kernel(_, own_ref, *rest):
        *other_refs, out_ref = rest
        total = own_ref[...]
        for r in other_refs:
            total += r[...].astype(jnp.float32)
        out_ref[0] = total.astype(out_ref.dtype)

    return pl.pallas_call(
        kernel,
        grid=(1,),
        in_specs=[ORDER] + [VMEM] * (1 + len(others)),
        out_specs=pl.BlockSpec((1, share, width), lambda i: (points - 1, 0, 0)),
        out_shape=jax.ShapeDtypeStruct(ready.shape, ready.dtype),
        input_output_aliases={0: 0},
        compiler_params=params(),
        cost_estimate=CHEAP,
        name="place_last",
    )(ready, own, *others)


def exchange(own, send):
    for d in range(1, send.shape[0] + 1):
        own += shifted(send[d - 1], "rows", d).astype(jnp.float32)
    return own


def per_device(coeffs, counts, kinetic, pair_table, trial_vecs, owner_map):
    points, radial, kept = coeffs.shape
    share, width = trial_vecs.shape[1:]
    blocks = owner_map.shape[0]
    me = lax.axis_index("rows").astype(jnp.int32).reshape(1)
    facts = jnp.concatenate([me, counts, owner_map])
    unit = radial // 12
    plain, tail = 4 * unit, 2 * unit
    mixed_rows = radial - plain
    peers = range(1, blocks)

    pieces = [[v] + [shifted(v, "rows", d) for d in peers] for v in parted(trial_vecs)]
    first = apply_first(coeffs, pieces[0], facts, mixed_rows, plain)
    first_sent = shifted(first, "blk", 1)

    table_index = jnp.arange(kinetic.shape[0], dtype=jnp.int32)
    one_hot = pair_table[:, :, None] == table_index[None, None, :]
    kin_own = jnp.sum(jnp.where(one_hot, kinetic[None, None, :], 0.0), axis=2)
    rest = apply_rest(coeffs, pieces, first, facts, mixed_rows, plain)
    rest_sent = shifted(rest, "blk", 1)
    kin_next = shifted(after(kin_own, rest, first_sent), "blk", -1)
    mixed = combine(coeffs, pieces, facts, kin_next, mixed_rows, tail, tail)
    mixed_sent = []
    previous = rest
    for z in mixed:
        z = after(z, previous)
        previous = z
        mixed_sent.append(shifted(z, "blk", 1))

    base = collect(coeffs, first_sent, rest_sent, kin_own, mixed_rows, plain)
    done = []
    earlier = first_sent
    for a in range(points - 1):
        own, send = finish_rows(
            coeffs, mixed_sent[a], base, earlier, facts, a, mixed_rows // 2, share
        )
        earlier = own
        done.append(exchange(own, send))
    last = points - 1
    total = gather_rows(coeffs, mixed_sent[last], base, earlier, last, mixed_rows - tail)
    ready = jnp.stack(done + done[:1]).astype(jnp.bfloat16)
    own, send = finish_last(
        coeffs[last, mixed_rows - tail : mixed_rows], mixed_sent[points], total, ready, facts, last, points, share
    )
    return place_last(ready, own, [shifted(send[d - 1], "rows", d) for d in peers])


def solution(mesh):
    in_specs = (P("blk", "rows", None), P("blk"), P(), P("blk", None), P("blk", "rows", None), P())
    out_specs = P("blk", "rows", None)
    return jax.shard_map(
        per_device, mesh=mesh, in_specs=in_specs, out_specs=out_specs, check_vma=False
    )
```

```python
import functools

import jax
import jax.numpy as jnp
from jax import lax
from jax.experimental import pallas as pl
from jax.experimental.pallas import tpu as pltpu
from jax.sharding import PartitionSpec as P

VMEM_LIMIT = 50 * 1024 * 1024
SMEM = pl.BlockSpec(memory_space=pltpu.SMEM)
VMEM = pl.BlockSpec(memory_space=pltpu.VMEM)
ORDER = pl.BlockSpec(memory_space=pl.ANY)
CHEAP = pl.CostEstimate(flops=1, bytes_accessed=1, transcendentals=0)


def shifted(block, axis, distance):
    devices = range(lax.axis_size(axis))
    route = [(i, (i + distance) % len(devices)) for i in devices]
    return lax.ppermute(block, axis, route)


def after(value, *others):
    return lax.optimization_barrier((value, *others))[0]


def params():
    return pltpu.CompilerParams(vmem_limit_bytes=VMEM_LIMIT)


def contract_rows(left, right):
    return lax.dot_general(
        left, right, (((0,), (0,)), ((), ())), preferred_element_type=jnp.float32
    )


def fill(vectors, pieces, count, me):
    share = pieces[0].shape[0]
    blocks = len(pieces)
    for d, piece in enumerate(pieces):
        start = pl.multiple_of(lax.rem(me + (blocks - d), blocks) * share, 16)
        row = start + lax.broadcasted_iota(jnp.int32, piece.shape, 0)
        kept = jnp.where(row < count, piece.astype(jnp.float32), 0.0)
        vectors[pl.ds(start, share), :] = kept.astype(vectors.dtype)


def parcels(points):
    return 1, points - 1


def place(point, sizes):
    for index, size in enumerate(sizes):
        if point < size:
            return index, point
        point -= size
    raise ValueError(point)


def part_of(vectors, first, size, *earlier):
    share, width = vectors.shape[1:]

    def kernel(vectors_ref, *rest):
        out_ref, sem = rest[-2:]
        copy = pltpu.make_async_copy(vectors_ref.at[pl.ds(first, size)], out_ref, sem)
        copy.start()
        copy.wait()

    return pl.pallas_call(
        kernel,
        in_specs=[ORDER] * (1 + len(earlier)),
        out_specs=VMEM,
        out_shape=jax.ShapeDtypeStruct((size, share, width), vectors.dtype),
        scratch_shapes=[pltpu.SemaphoreType.DMA],
        compiler_params=params(),
        cost_estimate=CHEAP,
        name="part_of",
    )(vectors, *earlier)


def fetch(sets, earlier, point, start, rows):
    kept = sets.shape[2]

    def kernel(sets_ref, _, block_ref, sem):
        copy = pltpu.make_async_copy(sets_ref.at[point, pl.ds(start, rows), :], block_ref, sem)
        copy.start()
        copy.wait()

    return pl.pallas_call(
        kernel,
        in_specs=[ORDER, ORDER],
        out_specs=VMEM,
        out_shape=jax.ShapeDtypeStruct((rows, kept), sets.dtype),
        scratch_shapes=[pltpu.SemaphoreType.DMA],
        compiler_params=params(),
        cost_estimate=CHEAP,
        name="fetch",
    )(sets, earlier)


def apply_first(sets, pieces, facts):
    rows, kept = sets.shape
    width = pieces[0].shape[2]

    def kernel(facts_ref, sets_ref, *rest):
        *piece_refs, out_ref, vectors = rest
        fill(vectors, [r[0] for r in piece_refs], facts_ref[1], facts_ref[0])
        out_ref[0] = jnp.dot(
            sets_ref[...], vectors[...], preferred_element_type=jnp.float32
        ).astype(out_ref.dtype)

    return pl.pallas_call(
        kernel,
        in_specs=[SMEM] + [VMEM] * (1 + len(pieces)),
        out_specs=VMEM,
        out_shape=jax.ShapeDtypeStruct((1, rows, width), jnp.bfloat16),
        scratch_shapes=[pltpu.VMEM((kept, width), jnp.bfloat16)],
        compiler_params=params(),
        cost_estimate=pl.CostEstimate(flops=10**9, bytes_accessed=10**6, transcendentals=0),
        name="apply_first",
    )(facts, sets, *pieces)


def apply_rest(sets, second, pieces, facts, start):
    points, _, kept = sets.shape
    rows = second.shape[0]
    width = pieces[0][0].shape[2]
    blocks = len(pieces[0])
    sizes = parcels(points)

    def kernel(facts_ref, sets_ref, second_ref, *rest):
        *piece_refs, out_ref, vectors, held, sems = rest
        copies = [
            pltpu.make_async_copy(
                sets_ref.at[j, pl.ds(start, rows), :], held.at[j - 2], sems.at[j - 2]
            )
            for j in range(2, points)
        ]
        for copy in copies:
            copy.start()
        for j in range(1, points):
            index, row = place(j, sizes)
            mine = piece_refs[index * blocks :][:blocks]
            fill(vectors, [r[row] for r in mine], facts_ref[1 + j], facts_ref[0])
            if j > 1:
                copies[j - 2].wait()
            block = second_ref[...] if j == 1 else held[j - 2]
            out_ref[j - 1] = jnp.dot(
                block, vectors[...], preferred_element_type=jnp.float32
            ).astype(out_ref.dtype)

    return pl.pallas_call(
        kernel,
        in_specs=[SMEM, ORDER, VMEM] + [VMEM] * (len(sizes) * blocks),
        out_specs=VMEM,
        out_shape=jax.ShapeDtypeStruct((points - 1, rows, width), jnp.bfloat16),
        scratch_shapes=[
            pltpu.VMEM((kept, width), jnp.bfloat16),
            pltpu.VMEM((points - 2, rows, kept), sets.dtype),
            pltpu.SemaphoreType.DMA((points - 2,)),
        ],
        compiler_params=params(),
        cost_estimate=CHEAP,
        name="apply_rest",
    )(facts, sets, second, *sum(pieces, []))


def combine(sets, pieces, facts, kin, length, block, tail):
    points, _, kept = sets.shape
    width = pieces[0][0].shape[2]
    sizes = parcels(points)
    steps = length // block
    body = steps - tail // block
    blocks = len(pieces[0])

    def kernel(facts_ref, kin_ref, sets_ref, *refs):
        used = len(sizes) * blocks
        piece_refs = refs[:used]
        outs, vectors = refs[used:-1], refs[-1]
        i = pl.program_id(0)

        @pl.when(i == 0)
        def _():
            for j in range(points):
                index, row = place(j, sizes)
                mine = piece_refs[index * blocks :][:blocks]
                fill(vectors.at[j], [r[row] for r in mine], facts_ref[1 + j], facts_ref[0])

        products = [
            jnp.dot(sets_ref[j], vectors[j], preferred_element_type=jnp.float32)
            for j in range(points)
        ]

        def mixed(a):
            total = kin_ref[a, 0] * products[0]
            for j in range(1, points):
                total += kin_ref[a, j] * products[j]
            return total.astype(jnp.bfloat16)

        for a in range(points - 1):
            outs[a][...] = mixed(a)
        last = mixed(points - 1)

        @pl.when(i < body)
        def _():
            outs[points - 1][...] = last

        @pl.when(i >= body)
        def _():
            outs[points][...] = last

    whole = pl.BlockSpec((block, width), lambda i: (i, 0))
    return pl.pallas_call(
        kernel,
        grid=(steps,),
        in_specs=[SMEM, SMEM, pl.BlockSpec((points, block, kept), lambda i: (0, i, 0))]
        + [VMEM] * (len(sizes) * blocks),
        out_specs=[whole] * (points - 1)
        + [
            pl.BlockSpec((block, width), lambda i: (jnp.minimum(i, body - 1), 0)),
            pl.BlockSpec((block, width), lambda i: (jnp.maximum(i - body, 0), 0)),
        ],
        out_shape=[jax.ShapeDtypeStruct((length, width), jnp.bfloat16)] * (points - 1)
        + [
            jax.ShapeDtypeStruct((length - tail, width), jnp.bfloat16),
            jax.ShapeDtypeStruct((tail, width), jnp.bfloat16),
        ],
        scratch_shapes=[pltpu.VMEM((points, kept, width), jnp.bfloat16)],
        compiler_params=params(),
        cost_estimate=CHEAP,
        name="combine",
    )(facts, kin, sets, *sum(pieces, []))


def collect(sets, first, rest, kin, start, rows):
    points, _, kept = sets.shape
    width = first.shape[2]
    skip = start // rows

    def kernel(kin_ref, sets_ref, first_ref, rest_ref, out_ref):
        a = pl.program_id(0)
        arrived = [first_ref[0]] + [rest_ref[j] for j in range(points - 1)]
        products = contract_rows(sets_ref[0], jnp.concatenate(arrived, axis=1))
        total = kin_ref[a, 0] * products[:, :width]
        for j in range(1, points):
            total += kin_ref[a, j] * products[:, j * width : (j + 1) * width]
        out_ref[0] = total

    return pl.pallas_call(
        kernel,
        grid=(points,),
        in_specs=[SMEM, pl.BlockSpec((1, rows, kept), lambda a: (a, skip, 0)), VMEM, VMEM],
        out_specs=pl.BlockSpec((1, kept, width), lambda a: (a, 0, 0)),
        out_shape=jax.ShapeDtypeStruct((points, kept, width), jnp.float32),
        compiler_params=params(),
        cost_estimate=CHEAP,
        name="collect",
    )(kin, sets, first, rest)


def split_blocks(total, point, points, facts_ref, held, own_ref, send_ref):
    blocks = facts_ref.shape[0] - 1 - points
    share = own_ref.shape[0]
    row = lax.broadcasted_iota(jnp.int32, total.shape, 0)
    held[...] = jnp.where(row < facts_ref[1 + point], total, 0.0)
    for d in range(blocks):
        start = pl.multiple_of(facts_ref[1 + points + lax.rem(facts_ref[0] + d, blocks)] * share, 16)
        part = held[pl.ds(start, share), :]
        if d == 0:
            own_ref[...] = part
        else:
            send_ref[d - 1] = part.astype(send_ref.dtype)


def gather_rows(sets, arrived, before, earlier, point, block):
    kept = sets.shape[2]
    length, width = arrived.shape

    def kernel(_, sets_ref, arrived_ref, before_ref, out_ref):
        @pl.when(pl.program_id(0) == 0)
        def _():
            out_ref[...] = before_ref[0]

        out_ref[...] += contract_rows(sets_ref[0], arrived_ref[...])

    return pl.pallas_call(
        kernel,
        grid=(length // block,),
        in_specs=[
            ORDER,
            pl.BlockSpec((1, block, kept), lambda i: (point, i, 0)),
            pl.BlockSpec((block, width), lambda i: (i, 0)),
            pl.BlockSpec((1, kept, width), lambda i: (point, 0, 0)),
        ],
        out_specs=pl.BlockSpec((kept, width), lambda i: (0, 0)),
        out_shape=jax.ShapeDtypeStruct((kept, width), jnp.float32),
        compiler_params=params(),
        cost_estimate=CHEAP,
        name="gather_rows",
    )(earlier, sets, arrived, before)


def finish_rows(sets, arrived, before, earlier, facts, point, block, share):
    points, _, kept = sets.shape
    length, width = arrived.shape
    steps = length // block
    blocks = facts.shape[0] - 1 - points

    def kernel(_, facts_ref, sets_ref, arrived_ref, before_ref, own_ref, send_ref, total, held):
        i = pl.program_id(0)

        @pl.when(i == 0)
        def _():
            total[...] = before_ref[0]

        total[...] += contract_rows(sets_ref[0], arrived_ref[...])

        @pl.when(i == steps - 1)
        def _():
            split_blocks(total[...], point, points, facts_ref, held, own_ref, send_ref)

    return pl.pallas_call(
        kernel,
        grid=(steps,),
        in_specs=[
            ORDER,
            SMEM,
            pl.BlockSpec((1, block, kept), lambda i: (point, i, 0)),
            pl.BlockSpec((block, width), lambda i: (i, 0)),
            pl.BlockSpec((1, kept, width), lambda i: (point, 0, 0)),
        ],
        out_specs=[
            pl.BlockSpec((share, width), lambda i: (0, 0)),
            pl.BlockSpec((blocks - 1, share, width), lambda i: (0, 0, 0)),
        ],
        out_shape=[
            jax.ShapeDtypeStruct((share, width), jnp.float32),
            jax.ShapeDtypeStruct((blocks - 1, share, width), jnp.bfloat16),
        ],
        scratch_shapes=[pltpu.VMEM((kept, width), jnp.float32)] * 2,
        compiler_params=params(),
        cost_estimate=CHEAP,
        name="finish_rows",
    )(earlier, facts, sets, arrived, before)


def finish_last(sets, arrived, before, earlier, facts, point, points, share):
    kept = sets.shape[1]
    width = arrived.shape[1]
    blocks = facts.shape[0] - 1 - points

    def kernel(_, facts_ref, sets_ref, arrived_ref, before_ref, own_ref, send_ref, held):
        total = before_ref[...] + contract_rows(sets_ref[...], arrived_ref[...])
        split_blocks(total, point, points, facts_ref, held, own_ref, send_ref)

    return pl.pallas_call(
        kernel,
        in_specs=[ORDER, SMEM] + [VMEM] * 3,
        out_specs=[VMEM, VMEM],
        out_shape=[
            jax.ShapeDtypeStruct((share, width), jnp.float32),
            jax.ShapeDtypeStruct((blocks - 1, share, width), jnp.bfloat16),
        ],
        scratch_shapes=[pltpu.VMEM((kept, width), jnp.float32)],
        compiler_params=params(),
        cost_estimate=CHEAP,
        name="finish_last",
    )(earlier, facts, sets, arrived, before)


def place_last(ready, own, others):
    points, share, width = ready.shape

    def kernel(_, own_ref, *rest):
        *other_refs, out_ref = rest
        total = own_ref[...]
        for r in other_refs:
            total += r[...].astype(jnp.float32)
        out_ref[0] = total.astype(out_ref.dtype)

    return pl.pallas_call(
        kernel,
        grid=(1,),
        in_specs=[ORDER] + [VMEM] * (1 + len(others)),
        out_specs=pl.BlockSpec((1, share, width), lambda i: (points - 1, 0, 0)),
        out_shape=jax.ShapeDtypeStruct(ready.shape, ready.dtype),
        input_output_aliases={0: 0},
        compiler_params=params(),
        cost_estimate=CHEAP,
        name="place_last",
    )(ready, own, *others)


def exchange(own, send):
    for d in range(1, send.shape[0] + 1):
        own += shifted(send[d - 1], "rows", d).astype(jnp.float32)
    return own


def per_device(coeffs, counts, kinetic, pair_table, trial_vecs, owner_map):
    points, radial, kept = coeffs.shape
    share, width = trial_vecs.shape[1:]
    blocks = owner_map.shape[0]
    me = lax.axis_index("rows").astype(jnp.int32).reshape(1)
    facts = jnp.concatenate([me, counts, owner_map])
    unit = radial // 12
    plain, tail = 4 * unit, 2 * unit
    mixed_rows = radial - plain
    peers = range(1, blocks)

    early = part_of(trial_vecs, 0, 1)
    late = part_of(trial_vecs, 1, points - 1, early)
    first_sets = fetch(coeffs, late, 0, mixed_rows, plain)
    pieces = [[v] + [shifted(v, "rows", d) for d in peers] for v in (early, late)]
    first = apply_first(first_sets, pieces[0], facts)
    first_sent = shifted(first, "blk", 1)

    table_index = jnp.arange(kinetic.shape[0], dtype=jnp.int32)
    one_hot = pair_table[:, :, None] == table_index[None, None, :]
    kin_own = jnp.sum(jnp.where(one_hot, kinetic[None, None, :], 0.0), axis=2)
    second = fetch(coeffs, first, 1, mixed_rows, plain)
    rest = apply_rest(coeffs, second, pieces, facts, mixed_rows)
    rest_sent = shifted(rest, "blk", 1)
    kin_next = shifted(after(kin_own, rest, first_sent), "blk", -1)
    mixed = combine(coeffs, pieces, facts, kin_next, mixed_rows, tail, tail)
    mixed_sent = []
    previous = rest
    for z in mixed:
        z = after(z, previous)
        previous = z
        mixed_sent.append(shifted(z, "blk", 1))

    base = collect(coeffs, first_sent, rest_sent, kin_own, mixed_rows, plain)
    done = []
    earlier = first_sent
    for a in range(points - 1):
        own, send = finish_rows(
            coeffs, mixed_sent[a], base, earlier, facts, a, mixed_rows // 2, share
        )
        earlier = own
        done.append(exchange(own, send))
    last = points - 1
    total = gather_rows(coeffs, mixed_sent[last], base, earlier, last, mixed_rows - tail)
    ready = jnp.stack(done + done[:1]).astype(jnp.bfloat16)
    own, send = finish_last(
        coeffs[last, mixed_rows - tail : mixed_rows], mixed_sent[points], total, ready, facts, last, points, share
    )
    return place_last(ready, own, [shifted(send[d - 1], "rows", d) for d in peers])


def solution(mesh):
    in_specs = (P("blk", "rows", None), P("blk"), P(), P("blk", None), P("blk", "rows", None), P())
    out_specs = P("blk", "rows", None)
    return jax.shard_map(
        per_device, mesh=mesh, in_specs=in_specs, out_specs=out_specs, check_vma=False
    )
```

```python
import functools

import jax
import jax.numpy as jnp
from jax import lax
from jax.experimental import pallas as pl
from jax.experimental.pallas import tpu as pltpu
from jax.sharding import PartitionSpec as P

VMEM_LIMIT = 50 * 1024 * 1024
SMEM = pl.BlockSpec(memory_space=pltpu.SMEM)
VMEM = pl.BlockSpec(memory_space=pltpu.VMEM)
ORDER = pl.BlockSpec(memory_space=pl.ANY)
CHEAP = pl.CostEstimate(flops=1, bytes_accessed=1, transcendentals=0)


def shifted(block, axis, distance):
    devices = range(lax.axis_size(axis))
    route = [(i, (i + distance) % len(devices)) for i in devices]
    return lax.ppermute(block, axis, route)


def after(value, *others):
    return lax.optimization_barrier((value, *others))[0]


def params():
    return pltpu.CompilerParams(vmem_limit_bytes=VMEM_LIMIT)


def contract_rows(left, right):
    return lax.dot_general(
        left, right, (((0,), (0,)), ((), ())), preferred_element_type=jnp.float32
    )


def fill(vectors, pieces, count, me):
    share = pieces[0].shape[0]
    blocks = len(pieces)
    for d, piece in enumerate(pieces):
        start = pl.multiple_of(lax.rem(me + (blocks - d), blocks) * share, 16)
        row = start + lax.broadcasted_iota(jnp.int32, piece.shape, 0)
        kept = jnp.where(row < count, piece.astype(jnp.float32), 0.0)
        vectors[pl.ds(start, share), :] = kept.astype(vectors.dtype)


def chosen(rows, values, shape):
    result = values[0]
    for index in range(1, len(values)):
        result = jnp.where(jnp.broadcast_to(rows, shape) == index, values[index], result)
    return result


def fill_by(vectors, pieces, flags_ref, point):
    shape = pieces[0].shape
    share, blocks = shape[0], len(pieces)
    held = [piece.astype(jnp.float32) for piece in pieces]
    for p in range(blocks):
        value = chosen(flags_ref[0:1, :], [held[(m - p) % blocks] for m in range(blocks)], shape)
        row = p * share + lax.broadcasted_iota(jnp.int32, shape, 0)
        count = jnp.broadcast_to(flags_ref[1 + point : 2 + point, :], shape)
        kept = jnp.where(row < count, value, 0.0)
        vectors[p * share : (p + 1) * share, :] = kept.astype(vectors.dtype)


def parcels(points):
    return 1, points - 1


def place(point, sizes):
    for index, size in enumerate(sizes):
        if point < size:
            return index, point
        point -= size
    raise ValueError(point)


def part_of(vectors, first, size, *earlier):
    share, width = vectors.shape[1:]

    def kernel(vectors_ref, *rest):
        out_ref, sem = rest[-2:]
        copy = pltpu.make_async_copy(vectors_ref.at[pl.ds(first, size)], out_ref, sem)
        copy.start()
        copy.wait()

    return pl.pallas_call(
        kernel,
        in_specs=[ORDER] * (1 + len(earlier)),
        out_specs=VMEM,
        out_shape=jax.ShapeDtypeStruct((size, share, width), vectors.dtype),
        scratch_shapes=[pltpu.SemaphoreType.DMA],
        compiler_params=params(),
        cost_estimate=CHEAP,
        name="part_of",
    )(vectors, *earlier)


def fetch(sets, earlier, point, start, rows):
    kept = sets.shape[2]

    def kernel(sets_ref, _, block_ref, sem):
        copy = pltpu.make_async_copy(sets_ref.at[point, pl.ds(start, rows), :], block_ref, sem)
        copy.start()
        copy.wait()

    return pl.pallas_call(
        kernel,
        in_specs=[ORDER, ORDER],
        out_specs=VMEM,
        out_shape=jax.ShapeDtypeStruct((rows, kept), sets.dtype),
        scratch_shapes=[pltpu.SemaphoreType.DMA],
        compiler_params=params(),
        cost_estimate=CHEAP,
        name="fetch",
    )(sets, earlier)


def apply_first(sets, pieces, flags):
    rows, kept = sets.shape
    width = pieces[0].shape[2]

    def kernel(flags_ref, sets_ref, *rest):
        *piece_refs, out_ref, vectors = rest
        fill_by(vectors, [r[0] for r in piece_refs], flags_ref, 0)
        out_ref[0] = jnp.dot(
            sets_ref[...], vectors[...], preferred_element_type=jnp.float32
        ).astype(out_ref.dtype)

    return pl.pallas_call(
        kernel,
        in_specs=[VMEM] * (2 + len(pieces)),
        out_specs=VMEM,
        out_shape=jax.ShapeDtypeStruct((1, rows, width), jnp.bfloat16),
        scratch_shapes=[pltpu.VMEM((kept, width), jnp.bfloat16)],
        compiler_params=params(),
        cost_estimate=pl.CostEstimate(flops=10**9, bytes_accessed=10**6, transcendentals=0),
        name="apply_first",
    )(flags, sets, *pieces)


def apply_rest(sets, second, pieces, flags, start):
    points, _, kept = sets.shape
    rows = second.shape[0]
    width = pieces[0][0].shape[2]
    blocks = len(pieces[0])
    sizes = parcels(points)

    def kernel(flags_ref, sets_ref, second_ref, *rest):
        *piece_refs, out_ref, vectors, held, sems = rest
        copies = [
            pltpu.make_async_copy(
                sets_ref.at[j, pl.ds(start, rows), :], held.at[j - 2], sems.at[j - 2]
            )
            for j in range(2, points)
        ]
        for copy in copies:
            copy.start()
        for j in range(1, points):
            index, row = place(j, sizes)
            mine = piece_refs[index * blocks :][:blocks]
            fill_by(vectors, [r[row] for r in mine], flags_ref, j)
            if j > 1:
                copies[j - 2].wait()
            block = second_ref[...] if j == 1 else held[j - 2]
            out_ref[j - 1] = jnp.dot(
                block, vectors[...], preferred_element_type=jnp.float32
            ).astype(out_ref.dtype)

    return pl.pallas_call(
        kernel,
        in_specs=[VMEM, ORDER, VMEM] + [VMEM] * (len(sizes) * blocks),
        out_specs=VMEM,
        out_shape=jax.ShapeDtypeStruct((points - 1, rows, width), jnp.bfloat16),
        scratch_shapes=[
            pltpu.VMEM((kept, width), jnp.bfloat16),
            pltpu.VMEM((points - 2, rows, kept), sets.dtype),
            pltpu.SemaphoreType.DMA((points - 2,)),
        ],
        compiler_params=params(),
        cost_estimate=CHEAP,
        name="apply_rest",
    )(flags, sets, second, *sum(pieces, []))


def combine(sets, pieces, facts, kin, length, block, tail):
    points, _, kept = sets.shape
    width = pieces[0][0].shape[2]
    sizes = parcels(points)
    steps = length // block
    body = steps - tail // block
    blocks = len(pieces[0])

    def kernel(facts_ref, kin_ref, sets_ref, *refs):
        used = len(sizes) * blocks
        piece_refs = refs[:used]
        outs, vectors = refs[used:-1], refs[-1]
        i = pl.program_id(0)

        @pl.when(i == 0)
        def _():
            for j in range(points):
                index, row = place(j, sizes)
                mine = piece_refs[index * blocks :][:blocks]
                fill(vectors.at[j], [r[row] for r in mine], facts_ref[1 + j], facts_ref[0])

        products = [
            jnp.dot(sets_ref[j], vectors[j], preferred_element_type=jnp.float32)
            for j in range(points)
        ]

        def mixed(a):
            total = kin_ref[a, 0] * products[0]
            for j in range(1, points):
                total += kin_ref[a, j] * products[j]
            return total.astype(jnp.bfloat16)

        for a in range(points - 1):
            outs[a][...] = mixed(a)
        last = mixed(points - 1)

        @pl.when(i < body)
        def _():
            outs[points - 1][...] = last

        @pl.when(i >= body)
        def _():
            outs[points][...] = last

    whole = pl.BlockSpec((block, width), lambda i: (i, 0))
    return pl.pallas_call(
        kernel,
        grid=(steps,),
        in_specs=[SMEM, SMEM, pl.BlockSpec((points, block, kept), lambda i: (0, i, 0))]
        + [VMEM] * (len(sizes) * blocks),
        out_specs=[whole] * (points - 1)
        + [
            pl.BlockSpec((block, width), lambda i: (jnp.minimum(i, body - 1), 0)),
            pl.BlockSpec((block, width), lambda i: (jnp.maximum(i - body, 0), 0)),
        ],
        out_shape=[jax.ShapeDtypeStruct((length, width), jnp.bfloat16)] * (points - 1)
        + [
            jax.ShapeDtypeStruct((length - tail, width), jnp.bfloat16),
            jax.ShapeDtypeStruct((tail, width), jnp.bfloat16),
        ],
        scratch_shapes=[pltpu.VMEM((points, kept, width), jnp.bfloat16)],
        compiler_params=params(),
        cost_estimate=CHEAP,
        name="combine",
    )(facts, kin, sets, *sum(pieces, []))


def collect(sets, first, rest, kin, start, rows):
    points, _, kept = sets.shape
    width = first.shape[2]
    skip = start // rows

    def kernel(kin_ref, sets_ref, first_ref, rest_ref, out_ref):
        a = pl.program_id(0)
        arrived = [first_ref[0]] + [rest_ref[j] for j in range(points - 1)]
        products = contract_rows(sets_ref[0], jnp.concatenate(arrived, axis=1))
        total = kin_ref[a, 0] * products[:, :width]
        for j in range(1, points):
            total += kin_ref[a, j] * products[:, j * width : (j + 1) * width]
        out_ref[0] = total

    return pl.pallas_call(
        kernel,
        grid=(points,),
        in_specs=[SMEM, pl.BlockSpec((1, rows, kept), lambda a: (a, skip, 0)), VMEM, VMEM],
        out_specs=pl.BlockSpec((1, kept, width), lambda a: (a, 0, 0)),
        out_shape=jax.ShapeDtypeStruct((points, kept, width), jnp.float32),
        compiler_params=params(),
        cost_estimate=CHEAP,
        name="collect",
    )(kin, sets, first, rest)


def split_blocks(total, point, points, facts_ref, held, own_ref, send_ref):
    blocks = facts_ref.shape[0] - 1 - points
    share = own_ref.shape[0]
    row = lax.broadcasted_iota(jnp.int32, total.shape, 0)
    held[...] = jnp.where(row < facts_ref[1 + point], total, 0.0)
    for d in range(blocks):
        start = pl.multiple_of(facts_ref[1 + points + lax.rem(facts_ref[0] + d, blocks)] * share, 16)
        part = held[pl.ds(start, share), :]
        if d == 0:
            own_ref[...] = part
        else:
            send_ref[d - 1] = part.astype(send_ref.dtype)


def gather_rows(sets, arrived, before, earlier, point, block):
    kept = sets.shape[2]
    length, width = arrived.shape

    def kernel(_, sets_ref, arrived_ref, before_ref, out_ref):
        @pl.when(pl.program_id(0) == 0)
        def _():
            out_ref[...] = before_ref[0]

        out_ref[...] += contract_rows(sets_ref[0], arrived_ref[...])

    return pl.pallas_call(
        kernel,
        grid=(length // block,),
        in_specs=[
            ORDER,
            pl.BlockSpec((1, block, kept), lambda i: (point, i, 0)),
            pl.BlockSpec((block, width), lambda i: (i, 0)),
            pl.BlockSpec((1, kept, width), lambda i: (point, 0, 0)),
        ],
        out_specs=pl.BlockSpec((kept, width), lambda i: (0, 0)),
        out_shape=jax.ShapeDtypeStruct((kept, width), jnp.float32),
        compiler_params=params(),
        cost_estimate=CHEAP,
        name="gather_rows",
    )(earlier, sets, arrived, before)


def finish_rows(sets, arrived, before, earlier, facts, point, block, share):
    points, _, kept = sets.shape
    length, width = arrived.shape
    steps = length // block
    blocks = facts.shape[0] - 1 - points

    def kernel(_, facts_ref, sets_ref, arrived_ref, before_ref, own_ref, send_ref, total, held):
        i = pl.program_id(0)

        @pl.when(i == 0)
        def _():
            total[...] = before_ref[0]

        total[...] += contract_rows(sets_ref[0], arrived_ref[...])

        @pl.when(i == steps - 1)
        def _():
            split_blocks(total[...], point, points, facts_ref, held, own_ref, send_ref)

    return pl.pallas_call(
        kernel,
        grid=(steps,),
        in_specs=[
            ORDER,
            SMEM,
            pl.BlockSpec((1, block, kept), lambda i: (point, i, 0)),
            pl.BlockSpec((block, width), lambda i: (i, 0)),
            pl.BlockSpec((1, kept, width), lambda i: (point, 0, 0)),
        ],
        out_specs=[
            pl.BlockSpec((share, width), lambda i: (0, 0)),
            pl.BlockSpec((blocks - 1, share, width), lambda i: (0, 0, 0)),
        ],
        out_shape=[
            jax.ShapeDtypeStruct((share, width), jnp.float32),
            jax.ShapeDtypeStruct((blocks - 1, share, width), jnp.bfloat16),
        ],
        scratch_shapes=[pltpu.VMEM((kept, width), jnp.float32)] * 2,
        compiler_params=params(),
        cost_estimate=CHEAP,
        name="finish_rows",
    )(earlier, facts, sets, arrived, before)


def finish_last(sets, arrived, before, earlier, flags, point, points, share):
    kept = sets.shape[1]
    width = arrived.shape[1]
    blocks = kept // share

    def kernel(_, flags_ref, sets_ref, arrived_ref, before_ref, own_ref, send_ref):
        total = before_ref[...] + contract_rows(sets_ref[...], arrived_ref[...])
        row = lax.broadcasted_iota(jnp.int32, total.shape, 0)
        count = jnp.broadcast_to(flags_ref[1 + point : 2 + point, :], total.shape)
        total = jnp.where(row < count, total, 0.0)
        parts = [total[b * share : (b + 1) * share] for b in range(blocks)]
        owners = [flags_ref[1 + points + i : 2 + points + i, :] for i in range(blocks)]
        me = flags_ref[0:1, :]
        for d in range(blocks):
            owner = chosen(me, [owners[(m + d) % blocks] for m in range(blocks)], me.shape)
            part = chosen(owner, parts, parts[0].shape)
            if d == 0:
                own_ref[...] = part
            else:
                send_ref[d - 1] = part.astype(send_ref.dtype)

    return pl.pallas_call(
        kernel,
        in_specs=[ORDER] + [VMEM] * 4,
        out_specs=[VMEM, VMEM],
        out_shape=[
            jax.ShapeDtypeStruct((share, width), jnp.float32),
            jax.ShapeDtypeStruct((blocks - 1, share, width), jnp.bfloat16),
        ],
        compiler_params=params(),
        cost_estimate=CHEAP,
        name="finish_last",
    )(earlier, flags, sets, arrived, before)


def place_last(ready, own, others):
    points, share, width = ready.shape

    def kernel(_, own_ref, *rest):
        *other_refs, out_ref = rest
        total = own_ref[...]
        for r in other_refs:
            total += r[...].astype(jnp.float32)
        out_ref[0] = total.astype(out_ref.dtype)

    return pl.pallas_call(
        kernel,
        grid=(1,),
        in_specs=[ORDER] + [VMEM] * (1 + len(others)),
        out_specs=pl.BlockSpec((1, share, width), lambda i: (points - 1, 0, 0)),
        out_shape=jax.ShapeDtypeStruct(ready.shape, ready.dtype),
        input_output_aliases={0: 0},
        compiler_params=params(),
        cost_estimate=CHEAP,
        name="place_last",
    )(ready, own, *others)


def exchange(own, send):
    for d in range(1, send.shape[0] + 1):
        own += shifted(send[d - 1], "rows", d).astype(jnp.float32)
    return own


def per_device(coeffs, counts, kinetic, pair_table, trial_vecs, owner_map):
    points, radial, kept = coeffs.shape
    share, width = trial_vecs.shape[1:]
    blocks = owner_map.shape[0]
    me = lax.axis_index("rows").astype(jnp.int32).reshape(1)
    facts = jnp.concatenate([me, counts, owner_map])
    flags = jnp.broadcast_to(facts[:, None], (facts.shape[0], width))
    unit = radial // 12
    plain, tail = 4 * unit, 2 * unit
    mixed_rows = radial - plain
    peers = range(1, blocks)

    early = part_of(trial_vecs, 0, 1)
    late = part_of(trial_vecs, 1, points - 1, early)
    first_sets = fetch(coeffs, late, 0, mixed_rows, plain)
    pieces = [[v] + [shifted(v, "rows", d) for d in peers] for v in (early, late)]
    first = apply_first(first_sets, pieces[0], flags)
    first_sent = shifted(first, "blk", 1)

    table_index = jnp.arange(kinetic.shape[0], dtype=jnp.int32)
    one_hot = pair_table[:, :, None] == table_index[None, None, :]
    kin_own = jnp.sum(jnp.where(one_hot, kinetic[None, None, :], 0.0), axis=2)
    second = fetch(coeffs, first, 1, mixed_rows, plain)
    rest = apply_rest(coeffs, second, pieces, flags, mixed_rows)
    rest_sent = shifted(rest, "blk", 1)
    kin_next = shifted(after(kin_own, rest, first_sent), "blk", -1)
    mixed = combine(coeffs, pieces, facts, kin_next, mixed_rows, tail, tail)
    mixed_sent = []
    previous = rest
    for z in mixed:
        z = after(z, previous)
        previous = z
        mixed_sent.append(shifted(z, "blk", 1))

    base = collect(coeffs, first_sent, rest_sent, kin_own, mixed_rows, plain)
    done = []
    earlier = first_sent
    for a in range(points - 1):
        own, send = finish_rows(
            coeffs, mixed_sent[a], base, earlier, facts, a, mixed_rows // 2, share
        )
        earlier = own
        done.append(exchange(own, send))
    last = points - 1
    total = gather_rows(coeffs, mixed_sent[last], base, earlier, last, mixed_rows - tail)
    ready = jnp.stack(done + done[:1]).astype(jnp.bfloat16)
    own, send = finish_last(
        coeffs[last, mixed_rows - tail : mixed_rows], mixed_sent[points], total, ready, flags, last, points, share
    )
    return place_last(ready, own, [shifted(send[d - 1], "rows", d) for d in peers])


def solution(mesh):
    in_specs = (P("blk", "rows", None), P("blk"), P(), P("blk", None), P("blk", "rows", None), P())
    out_specs = P("blk", "rows", None)
    return jax.shard_map(
        per_device, mesh=mesh, in_specs=in_specs, out_specs=out_specs, check_vma=False
    )
```
